32 devices in a mesh: grp: 2 (over x), tile: 8 (over z, y), tm: 2 (over core).
Axes of the slice: x: 2, y: 2, z: 4, core: 2. Of those that a mesh axis runs over, the one named last changes fastest.
Arguments:
- forcing: bfloat16 [24, 64, 32, 1024], P('tm', 'tile', 'grp'), parts along dimension 2, may hold values from -6 to 6
- first_weight: bfloat16 [3, 3, 16, 64], replicated, may hold values from -0.5 to 0.5
- second_weight: bfloat16 [3, 3, 64, 64], replicated, may hold values from -0.25 to 0.25
- head_weight: bfloat16 [64], replicated, may hold values from -0.75 to 0.75
- flow_codes: int32 [128, 1024], P('grp', 'tile'), parts along dimension 0, may hold values from 0 to 3, as said below
- outlet_cells: int32 [8, 64], P('tile', 'grp'), parts along dimension 1, may hold values from 127 to 8191, as said below
- receivers: int32 [8, 64], P('tile', 'grp'), parts along dimension 1, may hold values from -1 to 7, as said below
- inlet_cells: int32 [8, 64], P('tile', 'grp'), parts along dimension 1, may hold values from -1 to 8191, as said below
- levels: int32 [16], P(('grp', 'tile')), parts along dimension 0, may hold values from 0 to 7, as said below
Outputs:
- runoff: bfloat16 [24, 128, 1024], P('tm', 'grp', 'tile'), parts along dimension 1
- discharge: float32 [8, 64, 24], P('tile', 'grp', 'tm'), parts along dimension 1
The draws below stay inside these ranges and needn't reach their ends.
There are 2 independent parts, one for each index of `grp`. The reference program is written for one: setup_inputs(seed, part) draws one part's arguments, and reference() takes and returns one part's arrays. A program takes and returns all parts, laid end to end along the dimension named above; an argument that names none is the same for every part. Nothing has to cross between parts.
Inputs may be any that keep to these rules, and one draw needn't show every extreme that they name: `flow_codes`: in the last row of every tile each code is 0; elsewhere codes are 1, 2 or 3. `outlet_cells`: A tile's outlets are distinct cells of its last row; the last column's cell is always one. `receivers`: each outlet of a tile of level p below 7 sends to a tile of level p + 1; outlets of top-level tiles send to -1. `inlet_cells`: -1 exactly where receivers is -1. `levels`: every level holds 1 tiles.
All inputs are finite; a program needn't handle non-finite values.
Results may differ from the reference program's by a relative error of at most 0.0034.
Values may be sent and summed in bfloat16 or wider, within the bound.
A program may use at most 128 MiB of HBM per device.

```python
import jax
import jax.numpy as jnp
from jax import lax

TH = 128
TW = 64
CIN = 16
C = 64
NOUT = 32
LEVELS = 8
TILES = 8
NR = 1024
STEPS = 24


def route_tables(key):
    order = jax.random.permutation(jax.random.fold_in(key, 17), TILES).astype(jnp.int32)
    tile_levels = order % LEVELS
    inverse = jnp.argsort(order).astype(jnp.int32)
    picks = jax.random.randint(jax.random.fold_in(key, 19), (TILES, NOUT), 0, TILES // LEVELS)
    wanted = tile_levels[:, None] + 1 + LEVELS * picks
    at_top = tile_levels[:, None] == LEVELS - 1
    chosen = inverse[jnp.where(at_top, 0, wanted)]
    targets = jnp.where(at_top, -1, chosen).astype(jnp.int32)
    entry_cells = jax.random.randint(jax.random.fold_in(key, 23), (TILES, NOUT), 0, TH * TW)
    first_slot = lax.broadcasted_iota(jnp.int32, (TILES, NOUT), 1) == 0
    entry_cells = jnp.where(first_slot, TH * TW - 1, entry_cells)
    entry_cells = jnp.where(at_top, -1, entry_cells).astype(jnp.int32)
    return (tile_levels.astype(jnp.int32), targets, entry_cells)


def draw_flow_codes(key, part):
    row_ids = lax.broadcasted_iota(jnp.int32, (TW, NR), 1)
    codes = jax.random.randint(jax.random.fold_in(key, 11), (TW, NR), 1, 4)
    return jnp.where(row_ids % TH == TH - 1, 0, codes).astype(jnp.int32)


def draw_outlet_cells(key, part):
    keys = jax.random.split(jax.random.fold_in(key, 13), TILES)
    columns = jax.vmap(lambda sub_key: jax.random.permutation(sub_key, TW - 1))(keys)[:, :NOUT - 1]
    last_column = jnp.full((TILES, 1), TW - 1, jnp.int32)
    columns = jnp.concatenate([columns.astype(jnp.int32), last_column], axis=1)
    return (columns * TH + TH - 1).astype(jnp.int32)


def draw_receivers(key, part):
    return route_tables(key)[1]


def draw_inlet_cells(key, part):
    return route_tables(key)[2]


def draw_levels(key, part):
    return route_tables(key)[0]


def shard_levels(rng, dims, cuts, least, top_value):
    level = 1.0
    for position, shards_of in cuts:
        steps = jax.random.uniform(jax.random.fold_in(jax.random.fold_in(rng, 6), position), (shards_of,), jnp.float32, least / len(cuts), top_value / len(cuts))
        level = level * jnp.repeat(jnp.exp(steps), dims[position] // shards_of).reshape((-1,) + (1,) * (len(dims) - 1 - position))
    return level


def normal_values(own_key, extent, deviation, limit, shards=(), held_as=jnp.bfloat16):
    result = deviation * jax.random.normal(own_key, extent, jnp.float32)
    if shards:
        result = result * shard_levels(own_key, extent, shards, -0.22, 0.18)
    return jnp.clip(result, -limit, limit).astype(held_as)


def setup_inputs(seed: int = 0, part: int = 0) -> dict:
    splits = jax.random.split(jax.random.key(seed), 10)
    part_keys = jax.random.split(jax.random.fold_in(splits[9], part), 10)
    forcing = normal_values(part_keys[0], (STEPS, TW, CIN, NR), 1.0, 6.0, ((0, 2), (1, 8)))
    first_weight = normal_values(splits[1], (3, 3, CIN, C), (9 * CIN) ** -0.5, 0.5)
    second_weight = normal_values(splits[2], (3, 3, C, C), (9 * C) ** -0.5, 0.25)
    head_weight = normal_values(splits[3], (C,), C ** -0.5, 0.75)
    flow_codes = draw_flow_codes(jax.random.fold_in(jax.random.fold_in(splits[9], part), 71), part)
    outlet_cells = draw_outlet_cells(jax.random.fold_in(jax.random.fold_in(splits[9], part), 71), part)
    receivers = draw_receivers(jax.random.fold_in(jax.random.fold_in(splits[9], part), 71), part)
    inlet_cells = draw_inlet_cells(jax.random.fold_in(jax.random.fold_in(splits[9], part), 71), part)
    levels = draw_levels(jax.random.fold_in(jax.random.fold_in(splits[9], part), 71), part)
    return dict(forcing=forcing, first_weight=first_weight, second_weight=second_weight, head_weight=head_weight, flow_codes=flow_codes, outlet_cells=outlet_cells, receivers=receivers, inlet_cells=inlet_cells, levels=levels)


column_moves = (1, 1, 0, -1, -1, -1, 0, 1)
row_moves = (0, 1, 1, 1, 0, -1, -1, -1)


def lookup_table(direction, table):
    running = jnp.zeros(direction.shape, jnp.int32)
    for code_value in range(8):
        running = running + jnp.where(direction == code_value, table[code_value], 0).astype(jnp.int32)
    return running


def drain_roots(direction, outlets):
    column_ids = lax.broadcasted_iota(jnp.int32, (TW, TH), 0)
    row_ids = lax.broadcasted_iota(jnp.int32, (TW, TH), 1)
    new_column = column_ids + lookup_table(direction, column_moves)
    new_row = row_ids + lookup_table(direction, row_moves)
    inside = (new_column >= 0) & (new_column < TW) & (new_row >= 0) & (new_row < TH)
    own_cells = (column_ids * TH + row_ids).reshape(-1)
    moved = jnp.where(inside, new_column * TH + new_row, column_ids * TH + row_ids).reshape(-1)
    is_outlet = jnp.any(own_cells[:, None] == outlets[None, :], axis=1)
    moved = jnp.where(is_outlet, own_cells, moved).astype(jnp.int32)
    for turn_index in range((TW + TH).bit_length()):
        moved = moved[moved]
    return moved


def reference(forcing, first_weight, second_weight, head_weight, flow_codes, outlet_cells, receivers, inlet_cells, levels):
    first_kernel = first_weight.astype(jnp.float32).transpose(3, 2, 0, 1)
    second_kernel = second_weight.astype(jnp.float32).transpose(3, 2, 0, 1)
    head_values = head_weight.astype(jnp.float32)

    def step_runoff(one_step):
        inputs = one_step.astype(jnp.float32).transpose(1, 0, 2)[None]
        hidden = lax.conv_general_dilated(inputs, first_kernel, (1, 1), "SAME", precision=lax.Precision.HIGHEST)
        hidden = jnp.maximum(hidden, 0.0).astype(jnp.bfloat16)
        hidden = lax.optimization_barrier(hidden).astype(jnp.float32)
        deep = lax.conv_general_dilated(hidden, second_kernel, (1, 1), "SAME", precision=lax.Precision.HIGHEST)
        deep = jnp.maximum(deep[0], 0.0)
        logits = jnp.sum(deep * head_values[:, None, None], axis=0)
        return jax.nn.softplus(logits).astype(jnp.bfloat16)

    runoff = lax.map(step_runoff, forcing)
    tile_codes = flow_codes.reshape(TW, TILES, TH).transpose(1, 0, 2)
    root_cells = jax.vmap(drain_roots)(tile_codes, outlet_cells)
    tile_runoff = runoff.reshape(STEPS, TW, TILES, TH).transpose(2, 0, 1, 3).reshape(TILES, STEPS, TW * TH)

    def tile_local(packed):
        cell_runoff, roots_here, outlets_here = packed
        member = (roots_here[:, None] == outlets_here[None, :]).astype(jnp.float32)
        return jnp.dot(cell_runoff.astype(jnp.float32), member, precision=lax.Precision.HIGHEST, preferred_element_type=jnp.float32).T

    local_flow = lax.map(tile_local, (tile_runoff, root_cells, outlet_cells))
    safe_tiles = jnp.maximum(receivers, 0).astype(jnp.int32)
    safe_cells = jnp.maximum(inlet_cells, 0).astype(jnp.int32)
    inlet_roots = root_cells[safe_tiles, safe_cells]
    receiver_outlets = outlet_cells[safe_tiles]
    matches = inlet_roots[:, :, None] == receiver_outlets
    found = jnp.any(matches, axis=2) & (receivers >= 0)
    outlet_ids = lax.broadcasted_iota(jnp.int32, matches.shape, 2)
    which = jnp.sum(jnp.where(matches, outlet_ids, 0), axis=2).astype(jnp.int32)
    targets = jnp.where(found, safe_tiles * NOUT + which, 0).astype(jnp.int32).reshape(-1)
    valid = found.reshape(-1)
    outflow = local_flow.reshape(TILES * NOUT, STEPS)
    record_levels = jnp.repeat(levels, NOUT)
    for level_now in range(LEVELS - 1):
        sending = ((record_levels == level_now) & valid)[:, None]
        contrib = jnp.where(sending, outflow, 0.0)
        outflow = outflow.at[targets].add(contrib)
    discharge = (outflow * (NOUT / (TW * TH))).reshape(TILES, NOUT, STEPS)
    return runoff, discharge
```

```python
from functools import partial

import jax
import jax.numpy as jnp
from jax import lax
from jax.experimental import pallas as pl
from jax.experimental.pallas import tpu as pltpu
from jax.sharding import PartitionSpec as P

LEVELS = 8
F32 = jnp.float32
BF16 = jnp.bfloat16
VMEM_BYTES = 56 * 1024 * 1024


def iota(shape, dim):
    return lax.broadcasted_iota(jnp.int32, shape, dim)


def as_column(row_value, count):
    spread = jnp.broadcast_to(row_value.astype(F32), (count, count))
    return jnp.sum(
        jnp.where(iota((count, count), 0) == iota((count, count), 1), spread, 0.0),
        axis=1,
        keepdims=True,
    )


def drain_kernel(codes_ref, outlets_ref, receivers_ref, inlets_ref, levels_ref, packed_ref):
    width, height = codes_ref.shape
    count = outlets_ref.shape[1]
    codes = codes_ref[...].astype(F32)
    codes = jnp.concatenate([codes, jnp.full((height - width, height), 2.0, F32)], axis=0)
    codes = codes.T.astype(jnp.int32)
    shape = (height, height)
    rows, columns = iota(shape, 0), iota(shape, 1)
    moved = columns + jnp.where(codes == 1, 1, 0) - jnp.where(codes == 3, 1, 0)
    moved = jnp.where((moved < 0) | (moved >= width), height - 1, moved)
    landing = jnp.where((rows == height - 1) | (columns >= width), columns, moved)
    reach = 1
    while reach < height:
        below = jnp.concatenate([landing[reach:], columns[:reach]], axis=0)
        landing = jnp.take_along_axis(below, landing, axis=1, mode="promise_in_bounds")
        reach *= 2
    outlet_columns = as_column(outlets_ref[...], count).astype(jnp.int32) // height
    lanes = iota((count, height), 1)
    ranked = jnp.where(
        outlet_columns >= lanes, outlet_columns * count + iota((count, height), 0), height * count
    )
    nearest = jnp.min(ranked.astype(F32), axis=0, keepdims=True).astype(jnp.int32)
    nearest = jnp.where(iota((1, height), 1) < width, nearest % count, -1)
    drained = jnp.take_along_axis(
        jnp.broadcast_to(nearest, shape), landing, axis=1, mode="promise_in_bounds"
    )
    packed_ref[:width, :] = drained.astype(F32).T[:width]
    lane = iota((count, height), 1)
    table = jnp.where(lane == 0, as_column(receivers_ref[...], count), 0.0)
    table = jnp.where(lane == 1, as_column(inlets_ref[...], count), table)
    table = jnp.where(lane == 2, levels_ref[0].astype(F32), table)
    packed_ref[width:, :] = table


def shifted(value):
    count = value.shape[1]
    lanes = iota(value.shape, 1)
    before = jnp.where(lanes == 0, 0.0, pltpu.roll(value, 1, 1))
    after = jnp.where(lanes == count - 1, 0.0, pltpu.roll(value, count - 1, 1))
    return before, value, after


def route_matrix(gathered_ref, width, count):
    tiles, depth, height = gathered_ref.shape
    everything = tiles * count
    table = gathered_ref[:, width:, :].reshape(everything, height)
    receiver = table[:, 0:1].astype(jnp.int32)
    inlet = table[:, 1:2].astype(jnp.int32)
    sends = (receiver >= 0) & (table[:, 2:3] < LEVELS - 1.0)
    inlet_column = jnp.maximum(inlet, 0) // height
    inlet_row = jnp.maximum(inlet, 0) % height
    drained = gathered_ref[:, :width, :].reshape(tiles * width, height).astype(BF16)
    picks = jnp.where(
        iota((everything, tiles * width), 1) == receiver * width + inlet_column, 1.0, 0.0
    ).astype(BF16)
    picked = jnp.dot(picks, drained, preferred_element_type=F32)
    entered = jnp.sum(
        jnp.where(iota(picked.shape, 1) == inlet_row, picked, 0.0), axis=1, keepdims=True
    ).astype(jnp.int32)
    target = jnp.where(sends & (entered >= 0), receiver * count + entered, -1)
    square = (everything, everything)
    hop = jnp.where(iota(square, 1) == target, 1.0, 0.0)
    passed = hop + jnp.where(iota(square, 0) == iota(square, 1), 1.0, 0.0)
    hops = 1
    hop = hop.astype(BF16)
    while 2 * hops < LEVELS:
        hop = jnp.dot(hop, hop, preferred_element_type=F32).astype(BF16)
        passed = passed + jnp.dot(passed.astype(BF16), hop, preferred_element_type=F32)
        hops *= 2
    return passed


def conv_kernel(
    count,
    group1,
    group2,
    before_ref,
    forcing_ref,
    after_ref,
    w1_ref,
    w2_ref,
    head_ref,
    gathered_ref,
    runoff_ref,
    flow_ref,
    x_ref,
    h_ref,
    s_ref,
):
    step = pl.program_id(0)
    place = lax.axis_index("tile")
    tiles = runoff_ref.shape[0]
    _, band, cin, rows = forcing_ref.shape
    height = runoff_ref.shape[3]
    channels = head_ref.shape[0]
    chunk = 256
    first = 0
    for ref in (before_ref, forcing_ref, after_ref):
        depth = ref.shape[1] * cin
        parts = shifted(ref[0].reshape(depth, rows).astype(F32))
        for b in range(3):
            x_ref[b, first : first + depth, :] = parts[b].astype(BF16)
        first += depth
    start = 0
    while start < band + 2:
        wide = min(group1, band + 2 - start)
        span = (wide + 2) * cin
        if wide == group1:
            weights = w1_ref[...]
        else:
            weights = jnp.concatenate(
                [
                    w1_ref[: wide * channels, b * (group1 + 2) * cin : b * (group1 + 2) * cin + span]
                    for b in range(3)
                ],
                axis=1,
            )
        source = jnp.concatenate(
            [x_ref[b, start * cin : start * cin + span, :] for b in range(3)], axis=0
        )
        result = jnp.maximum(jnp.dot(weights, source, preferred_element_type=F32), 0.0)
        for i in range(wide):
            piece = result[i * channels : (i + 1) * channels]
            if start + i == 0:
                piece = jnp.where(place == 0, 0.0, piece)
            if start + i == band + 1:
                piece = jnp.where(place == tiles - 1, 0.0, piece)
            parts = shifted(piece)
            at = (start + i) * channels
            for b in range(3):
                h_ref[b, at : at + channels, :] = parts[b].astype(BF16)
        start += wide
    head = head_ref[...]
    head = jnp.concatenate([head, head], axis=1)
    span = (group2 + 2) * channels
    logits = []
    for start in range(0, band, group2):
        at = start * channels
        pieces = []
        for lane in range(0, rows, chunk):
            source = jnp.concatenate(
                [h_ref[b, at : at + span, lane : lane + chunk] for b in range(3)], axis=0
            )
            deep = jnp.maximum(jnp.dot(w2_ref[...], source, preferred_element_type=F32), 0.0)
            pieces.append(
                jnp.concatenate(
                    [
                        jnp.sum(
                            deep[i * channels : (i + 1) * channels] * head, axis=0, keepdims=True
                        )
                        for i in range(group2)
                    ],
                    axis=0,
                )
            )
        logits.append(jnp.concatenate(pieces, axis=1))
    logits = jnp.concatenate(logits, axis=0)
    soft = jnp.maximum(logits, 0.0) + jnp.log1p(jnp.exp(-jnp.abs(logits)))
    rounded = soft.astype(BF16)
    for k in range(tiles):
        runoff_ref[k, 0] = rounded[:, k * height : (k + 1) * height]
    kept = rounded.astype(F32)
    for c in range(band):
        s_ref[c, pl.ds(step, 1), :] = kept[c : c + 1]

    @pl.when(step == pl.num_programs(0) - 1)
    def _():
        width = band * tiles
        depth = s_ref.shape[1]
        steps = s_ref[...].astype(BF16)
        sums = []
        for k in range(tiles):
            left, right = [], []
            own = gathered_ref[k, pl.ds(place * band, band), :].astype(jnp.int32)
            for c in range(band):
                left.append(steps[c, :, k * height : (k + 1) * height])
                right.append(
                    jnp.where(iota((count, height), 0) == own[c : c + 1], 1.0, 0.0).astype(BF16)
                )
            sums.append(
                lax.dot_general(
                    jnp.concatenate(left, axis=1),
                    jnp.concatenate(right, axis=1),
                    (((1,), (1,)), ((), ())),
                    preferred_element_type=F32,
                )
            )
        local = jnp.concatenate(sums, axis=1)
        local = jnp.where(iota(local.shape, 0) < pl.num_programs(0), local, 0.0)
        passed = route_matrix(gathered_ref, width, count)
        flow_ref[...] = jnp.dot(
            local, passed, precision=lax.Precision.HIGHEST, preferred_element_type=F32
        )


def banded(weight, group):
    cin, cout = weight.shape[2:]
    flat = jnp.transpose(weight, (3, 1, 0, 2))
    stacked = jnp.stack(
        [jnp.pad(flat, ((0, 0), (0, 0), (j, group - 1 - j), (0, 0))) for j in range(group)]
    )
    return stacked.reshape(group * cout, 3 * (group + 2) * cin)


def local(
    forcing,
    first_weight,
    second_weight,
    head_weight,
    flow_codes,
    outlet_cells,
    receivers,
    inlet_cells,
    levels,
):
    tiles = lax.axis_size("tile")
    step_count, band, cin, rows = forcing.shape
    width, height = flow_codes.shape
    count = outlet_cells.shape[1]
    channels = first_weight.shape[3]
    group1, group2 = 3, min(4, band)

    up = [(i, i + 1) for i in range(tiles - 1)]
    down = [(j, i) for i, j in up]
    before = lax.ppermute(lax.slice_in_dim(forcing, band - 2, band, axis=1), "tile", up)
    after = lax.ppermute(lax.slice_in_dim(forcing, 0, 2, axis=1), "tile", down)

    packed = pl.pallas_call(
        drain_kernel,
        out_shape=jax.ShapeDtypeStruct((width + count, height), F32),
        in_specs=[pl.BlockSpec(memory_space=pltpu.VMEM)] * 4
        + [pl.BlockSpec(memory_space=pltpu.SMEM)],
        out_specs=pl.BlockSpec(memory_space=pltpu.VMEM),
    )(flow_codes, outlet_cells, receivers, inlet_cells, levels)
    gathered = lax.all_to_all(
        jnp.broadcast_to(packed[None], (tiles,) + packed.shape), "tile", 0, 0, tiled=True
    )

    w1 = banded(first_weight, group1)
    w2 = banded(second_weight, group2)
    head = jnp.broadcast_to(head_weight.astype(F32)[:, None], (channels, 128))

    whole = lambda value: pl.BlockSpec(value.shape, lambda t: (0,) * value.ndim)
    per_step = lambda value: pl.BlockSpec((1,) + value.shape[1:], lambda t: (t, 0, 0, 0))
    padded_steps = -(-step_count // 16) * 16
    blocks, flows = pl.pallas_call(
        partial(conv_kernel, count, group1, group2),
        grid=(step_count,),
        in_specs=[
            per_step(before),
            per_step(forcing),
            per_step(after),
            whole(w1),
            whole(w2),
            whole(head),
            whole(gathered),
        ],
        out_shape=(
            jax.ShapeDtypeStruct((tiles, step_count, band, height), BF16),
            jax.ShapeDtypeStruct((padded_steps, tiles * count), F32),
        ),
        out_specs=(
            pl.BlockSpec((tiles, 1, band, height), lambda t: (0, t, 0, 0)),
            pl.BlockSpec((padded_steps, tiles * count), lambda t: (0, 0)),
        ),
        scratch_shapes=[
            pltpu.VMEM((3, (band + 4) * cin, rows), BF16),
            pltpu.VMEM((3, (band + 2) * channels, rows), BF16),
            pltpu.VMEM((band, padded_steps, rows), F32),
        ],
        compiler_params=pltpu.CompilerParams(vmem_limit_bytes=VMEM_BYTES),
    )(before, forcing, after, w1, w2, head, gathered)

    received = lax.all_to_all(blocks, "tile", 0, 0, tiled=True)
    runoff = jnp.transpose(received, (1, 0, 2, 3)).reshape(step_count, tiles * band, height)
    shares = flows[:step_count].reshape(step_count, tiles, count)
    shares = jnp.transpose(shares, (1, 2, 0))
    arrived = lax.all_to_all(shares, "tile", 0, 0, tiled=True)
    discharge = (jnp.sum(arrived, axis=0) * (count / (width * height)))[None]
    return (runoff, discharge)


def solution(mesh):
    placed = (
        P("tm", "tile", "grp", None),
        P(),
        P(),
        P(),
        P("grp", "tile"),
        P("tile", "grp"),
        P("tile", "grp"),
        P("tile", "grp"),
        P(("grp", "tile")),
    )
    return jax.shard_map(
        local,
        mesh=mesh,
        in_specs=placed,
        out_specs=(P("tm", "grp", "tile"), P("tile", "grp", "tm")),
        check_vma=False,
    )
```

```python
from functools import partial

import jax
import jax.numpy as jnp
from jax import lax
from jax.experimental import pallas as pl
from jax.experimental.pallas import tpu as pltpu
from jax.sharding import PartitionSpec as P

LEVELS = 8
F32 = jnp.float32
BF16 = jnp.bfloat16
VMEM_BYTES = 56 * 1024 * 1024


def iota(shape, dim):
    return lax.broadcasted_iota(jnp.int32, shape, dim)


def as_column(row_value, count):
    spread = jnp.broadcast_to(row_value.astype(F32), (count, count))
    return jnp.sum(
        jnp.where(iota((count, count), 0) == iota((count, count), 1), spread, 0.0),
        axis=1,
        keepdims=True,
    )


def drain_kernel(codes_ref, outlets_ref, receivers_ref, inlets_ref, levels_ref, packed_ref):
    width, height = codes_ref.shape
    count = outlets_ref.shape[1]
    codes = codes_ref[...].astype(F32)
    codes = jnp.concatenate([codes, jnp.full((height - width, height), 2.0, F32)], axis=0)
    codes = codes.T.astype(jnp.int32)
    shape = (height, height)
    rows, columns = iota(shape, 0), iota(shape, 1)
    moved = columns + jnp.where(codes == 1, 1, 0) - jnp.where(codes == 3, 1, 0)
    moved = jnp.where((moved < 0) | (moved >= width), height - 1, moved)
    landing = jnp.where((rows == height - 1) | (columns >= width), columns, moved)
    reach = 1
    while reach < height:
        below = jnp.concatenate([landing[reach:], columns[:reach]], axis=0)
        landing = jnp.take_along_axis(below, landing, axis=1, mode="promise_in_bounds")
        reach *= 2
    outlet_columns = as_column(outlets_ref[...], count).astype(jnp.int32) // height
    lanes = iota((count, height), 1)
    ranked = jnp.where(
        outlet_columns >= lanes, outlet_columns * count + iota((count, height), 0), height * count
    )
    nearest = jnp.min(ranked.astype(F32), axis=0, keepdims=True).astype(jnp.int32)
    nearest = jnp.where(iota((1, height), 1) < width, nearest % count, -1)
    drained = jnp.take_along_axis(
        jnp.broadcast_to(nearest, shape), landing, axis=1, mode="promise_in_bounds"
    )
    packed_ref[:width, :] = drained.astype(F32).T[:width]
    lane = iota((count, height), 1)
    table = jnp.where(lane == 0, as_column(receivers_ref[...], count), 0.0)
    table = jnp.where(lane == 1, as_column(inlets_ref[...], count), table)
    table = jnp.where(lane == 2, levels_ref[0].astype(F32), table)
    packed_ref[width:, :] = table


def shifted(value):
    count = value.shape[1]
    lanes = iota(value.shape, 1)
    before = jnp.where(lanes == 0, 0.0, pltpu.roll(value, 1, 1))
    after = jnp.where(lanes == count - 1, 0.0, pltpu.roll(value, count - 1, 1))
    return before, value, after


def route_matrix(gathered_ref, width, count):
    tiles, depth, height = gathered_ref.shape
    everything = tiles * count
    table = gathered_ref[:, width:, :].reshape(everything, height)
    receiver = table[:, 0:1].astype(jnp.int32)
    inlet = table[:, 1:2].astype(jnp.int32)
    sends = (receiver >= 0) & (table[:, 2:3] < LEVELS - 1.0)
    inlet_column = jnp.maximum(inlet, 0) // height
    inlet_row = jnp.maximum(inlet, 0) % height
    drained = gathered_ref[:, :width, :].reshape(tiles * width, height).astype(BF16)
    picks = jnp.where(
        iota((everything, tiles * width), 1) == receiver * width + inlet_column, 1.0, 0.0
    ).astype(BF16)
    picked = jnp.dot(picks, drained, preferred_element_type=F32)
    entered = jnp.sum(
        jnp.where(iota(picked.shape, 1) == inlet_row, picked, 0.0), axis=1, keepdims=True
    ).astype(jnp.int32)
    target = jnp.where(sends & (entered >= 0), receiver * count + entered, -1)
    square = (everything, everything)
    hop = jnp.where(iota(square, 1) == target, 1.0, 0.0)
    passed = hop + jnp.where(iota(square, 0) == iota(square, 1), 1.0, 0.0)
    hops = 1
    hop = hop.astype(BF16)
    while 2 * hops < LEVELS:
        hop = jnp.dot(hop, hop, preferred_element_type=F32).astype(BF16)
        passed = passed + jnp.dot(passed.astype(BF16), hop, preferred_element_type=F32)
        hops *= 2
    return passed


def lay_out(weight_ref, out_ref, group):
    cin, cout = weight_ref.shape[2:]
    same = jnp.where(iota((cout, cout), 0) == iota((cout, cout), 1), 1.0, 0.0).astype(BF16)
    for j in range(group):
        parts = []
        for b in range(3):
            if j > 0:
                parts.append(jnp.zeros((j * cin, cout), BF16))
            parts += [weight_ref[a, b] for a in range(3)]
            if j < group - 1:
                parts.append(jnp.zeros(((group - 1 - j) * cin, cout), BF16))
        out_ref[j * cout : (j + 1) * cout, :] = lax.dot_general(
            same,
            jnp.concatenate(parts, axis=0),
            (((1,), (1,)), ((), ())),
            preferred_element_type=F32,
        ).astype(BF16)


def one_step(
    step,
    place,
    tiles,
    group1,
    group2,
    before_ref,
    forcing_ref,
    after_ref,
    w1_ref,
    w2_ref,
    head_ref,
    x_ref,
    h_ref,
):
    _, band, cin, rows = forcing_ref.shape
    channels = head_ref.shape[0]
    chunk = 256
    first = 0
    for ref in (before_ref, forcing_ref, after_ref):
        depth = ref.shape[1] * cin
        parts = shifted(ref[step].reshape(depth, rows).astype(F32))
        for b in range(3):
            x_ref[b, first : first + depth, :] = parts[b].astype(BF16)
        first += depth
    start = 0
    while start < band + 2:
        wide = min(group1, band + 2 - start)
        span = (wide + 2) * cin
        if wide == group1:
            weights = w1_ref[...]
        else:
            weights = jnp.concatenate(
                [
                    w1_ref[: wide * channels, b * (group1 + 2) * cin : b * (group1 + 2) * cin + span]
                    for b in range(3)
                ],
                axis=1,
            )
        source = jnp.concatenate(
            [x_ref[b, start * cin : start * cin + span, :] for b in range(3)], axis=0
        )
        result = jnp.maximum(jnp.dot(weights, source, preferred_element_type=F32), 0.0)
        for i in range(wide):
            piece = result[i * channels : (i + 1) * channels]
            if start + i == 0:
                piece = jnp.where(place == 0, 0.0, piece)
            if start + i == band + 1:
                piece = jnp.where(place == tiles - 1, 0.0, piece)
            parts = shifted(piece)
            at = (start + i) * channels
            for b in range(3):
                h_ref[b, at : at + channels, :] = parts[b].astype(BF16)
        start += wide
    head = jnp.concatenate([head_ref[...]] * 2, axis=1)
    span = (group2 + 2) * channels
    logits = []
    for start in range(0, band, group2):
        at = start * channels
        pieces = []
        for lane in range(0, rows, chunk):
            source = jnp.concatenate(
                [h_ref[b, at : at + span, lane : lane + chunk] for b in range(3)], axis=0
            )
            deep = jnp.maximum(jnp.dot(w2_ref[...], source, preferred_element_type=F32), 0.0)
            pieces.append(
                jnp.concatenate(
                    [
                        jnp.sum(
                            deep[i * channels : (i + 1) * channels] * head, axis=0, keepdims=True
                        )
                        for i in range(group2)
                    ],
                    axis=0,
                )
            )
        logits.append(jnp.concatenate(pieces, axis=1))
    logits = jnp.concatenate(logits, axis=0)
    soft = jnp.maximum(logits, 0.0) + jnp.log1p(jnp.exp(-jnp.abs(logits)))
    return soft.astype(BF16)


def band_sums(place, count, gathered_ref, s_ref):
    tiles, _, height = gathered_ref.shape
    band = s_ref.shape[0]
    steps = s_ref[...].astype(BF16)
    sums = []
    for k in range(tiles):
        left, right = [], []
        own = gathered_ref[k, pl.ds(place * band, band), :].astype(jnp.int32)
        for c in range(band):
            left.append(steps[c, :, k * height : (k + 1) * height])
            right.append(
                jnp.where(iota((count, height), 0) == own[c : c + 1], 1.0, 0.0).astype(BF16)
            )
        sums.append(
            lax.dot_general(
                jnp.concatenate(left, axis=1),
                jnp.concatenate(right, axis=1),
                (((1,), (1,)), ((), ())),
                preferred_element_type=F32,
            )
        )
    return jnp.concatenate(sums, axis=1)


def main_kernel(
    count,
    group1,
    group2,
    forcing_ref,
    first_ref,
    second_ref,
    headrow_ref,
    packed_ref,
    runoff_ref,
    flow_ref,
    before_ref,
    after_ref,
    gathered_ref,
    w1_ref,
    w2_ref,
    head_ref,
    x_ref,
    h_ref,
    s_ref,
    out_ref,
    share_ref,
    landed_ref,
    halo_send,
    halo_recv,
    table_send,
    table_recv,
    runoff_send,
    runoff_recv,
    share_send,
    share_recv,
):
    place = lax.axis_index("tile")
    tiles, step_count, band, height = runoff_ref.shape
    batches = runoff_send.shape[0]
    per = step_count // batches

    def each_peer(act):
        def turn(d, carry):
            act(d, lax.rem(place + d, tiles), lax.rem(place + tiles - d, tiles))
            return carry

        lax.fori_loop(1, tiles, turn, 0)

    def remote(source, landing, send, recv, peer):
        return pltpu.make_async_remote_copy(
            src_ref=source,
            dst_ref=landing,
            send_sem=send,
            recv_sem=recv,
            device_id={"tile": peer},
            device_id_type=pl.DeviceIdType.MESH,
        )

    def halo_up(t):
        return remote(
            forcing_ref.at[t, pl.ds(band - 2, 2)],
            before_ref.at[t],
            halo_send.at[0, t],
            halo_recv.at[0, t],
            place + 1,
        )

    def halo_down(t):
        return remote(
            forcing_ref.at[t, pl.ds(0, 2)],
            after_ref.at[t],
            halo_send.at[1, t],
            halo_recv.at[1, t],
            place - 1,
        )

    def table(d, peer, slot):
        return remote(
            packed_ref, gathered_ref.at[slot], table_send.at[d], table_recv.at[d], peer
        )

    def runoff_part(g, d, peer, slot):
        return remote(
            out_ref.at[peer, pl.ds(g * per, per)],
            runoff_ref.at[slot, pl.ds(g * per, per)],
            runoff_send.at[g, d],
            runoff_recv.at[g, d],
            peer,
        )

    def share(d, peer, slot):
        return remote(
            share_ref.at[peer], landed_ref.at[slot], share_send.at[d], share_recv.at[d], peer
        )

    barrier = pltpu.get_barrier_semaphore()
    each_peer(
        lambda d, peer, source: pl.semaphore_signal(
            barrier, inc=1, device_id={"tile": peer}, device_id_type=pl.DeviceIdType.MESH
        )
    )
    pl.semaphore_wait(barrier, tiles - 1)

    def start_halos(t, carry):
        @pl.when(place < tiles - 1)
        def _():
            halo_up(t).start()

        @pl.when(place > 0)
        def _():
            halo_down(t).start()

        return carry

    lax.fori_loop(0, step_count, start_halos, 0)
    each_peer(lambda d, peer, source: table(d, peer, place).start())

    @pl.when(place == 0)
    def _():
        before_ref[...] = jnp.zeros_like(before_ref)

    @pl.when(place == tiles - 1)
    def _():
        after_ref[...] = jnp.zeros_like(after_ref)

    gathered_ref[place] = packed_ref[...]
    s_ref[...] = jnp.zeros_like(s_ref)
    lay_out(first_ref, w1_ref, group1)
    lay_out(second_ref, w2_ref, group2)
    channels = head_ref.shape[0]
    head_ref[...] = jnp.broadcast_to(as_column(headrow_ref[...], channels), head_ref.shape)

    def batch(g, carry):
        def turn(i, inner):
            t = g * per + i

            @pl.when(place > 0)
            def _():
                halo_up(t).wait_recv()

            @pl.when(place < tiles - 1)
            def _():
                halo_down(t).wait_recv()

            rounded = one_step(
                t,
                place,
                tiles,
                group1,
                group2,
                before_ref,
                forcing_ref,
                after_ref,
                w1_ref,
                w2_ref,
                head_ref,
                x_ref,
                h_ref,
            )
            for k in range(tiles):
                out_ref[k, t] = rounded[:, k * height : (k + 1) * height]
            kept = rounded.astype(F32)
            for c in range(band):
                s_ref[c, pl.ds(t, 1), :] = kept[c : c + 1]
            return inner

        lax.fori_loop(0, per, turn, 0)
        each_peer(lambda d, peer, source: runoff_part(g, d, peer, place).start())
        return carry

    lax.fori_loop(0, batches, batch, 0)
    runoff_ref[place] = out_ref[place]

    each_peer(lambda d, peer, source: table(d, peer, source).wait_recv())
    local_sums = band_sums(place, count, gathered_ref, s_ref)
    passed = route_matrix(gathered_ref, band * tiles, count)
    flows = jnp.dot(
        local_sums, passed, precision=lax.Precision.HIGHEST, preferred_element_type=F32
    )
    filler = jnp.zeros((flows.shape[0], share_ref.shape[2] - count), F32)
    for k in range(tiles):
        share_ref[k] = jnp.concatenate([flows[:, k * count : (k + 1) * count], filler], axis=1)
    each_peer(lambda d, peer, source: share(d, peer, place).start())
    landed_ref[place] = share_ref[place]
    each_peer(lambda d, peer, source: share(d, peer, source).wait_recv())
    scale = count / (band * tiles * height)
    flow_ref[...] = jnp.sum(landed_ref[...], axis=0) * scale

    def finish(g, carry):
        each_peer(lambda d, peer, source: runoff_part(g, d, peer, source).wait_recv())
        each_peer(lambda d, peer, source: runoff_part(g, d, peer, place).wait_send())
        return carry

    lax.fori_loop(0, batches, finish, 0)
    each_peer(lambda d, peer, source: share(d, peer, place).wait_send())
    each_peer(lambda d, peer, source: table(d, peer, place).wait_send())

    def end_halos(t, carry):
        @pl.when(place < tiles - 1)
        def _():
            halo_up(t).wait_send()

        @pl.when(place > 0)
        def _():
            halo_down(t).wait_send()

        return carry

    lax.fori_loop(0, step_count, end_halos, 0)


def local(
    forcing,
    first_weight,
    second_weight,
    head_weight,
    flow_codes,
    outlet_cells,
    receivers,
    inlet_cells,
    levels,
):
    tiles = lax.axis_size("tile")
    step_count, band, cin, rows = forcing.shape
    width, height = flow_codes.shape
    count = outlet_cells.shape[1]
    channels = first_weight.shape[3]
    group1, group2 = 3, min(4, band)

    packed = pl.pallas_call(
        drain_kernel,
        out_shape=jax.ShapeDtypeStruct((width + count, height), F32),
        in_specs=[pl.BlockSpec(memory_space=pltpu.VMEM)] * 4
        + [pl.BlockSpec(memory_space=pltpu.SMEM)],
        out_specs=pl.BlockSpec(memory_space=pltpu.VMEM),
    )(flow_codes, outlet_cells, receivers, inlet_cells, levels)
    padded_steps = -(-step_count // 16) * 16
    batches = step_count // 3 if step_count % 3 == 0 else step_count
    dma = pltpu.SemaphoreType.DMA
    vmem = pl.BlockSpec(memory_space=pltpu.VMEM)
    blocks, flows = pl.pallas_call(
        partial(main_kernel, count, group1, group2),
        in_specs=[vmem] * 5,
        out_shape=(
            jax.ShapeDtypeStruct((tiles, step_count, band, height), BF16),
            jax.ShapeDtypeStruct((padded_steps, 128), F32),
        ),
        out_specs=(vmem, vmem),
        scratch_shapes=[
            pltpu.VMEM((step_count, 2, cin, rows), BF16),
            pltpu.VMEM((step_count, 2, cin, rows), BF16),
            pltpu.VMEM((tiles, width + count, height), F32),
            pltpu.VMEM((group1 * channels, 3 * (group1 + 2) * cin), BF16),
            pltpu.VMEM((group2 * channels, 3 * (group2 + 2) * channels), BF16),
            pltpu.VMEM((channels, 128), F32),
            pltpu.VMEM((3, (band + 4) * cin, rows), BF16),
            pltpu.VMEM((3, (band + 2) * channels, rows), BF16),
            pltpu.VMEM((band, padded_steps, rows), F32),
            pltpu.VMEM((tiles, step_count, band, height), BF16),
            pltpu.VMEM((tiles, padded_steps, 128), F32),
            pltpu.VMEM((tiles, padded_steps, 128), F32),
            dma((2, step_count)),
            dma((2, step_count)),
            dma((tiles,)),
            dma((tiles,)),
            dma((batches, tiles)),
            dma((batches, tiles)),
            dma((tiles,)),
            dma((tiles,)),
        ],
        compiler_params=pltpu.CompilerParams(
            collective_id=0, has_side_effects=True, vmem_limit_bytes=VMEM_BYTES
        ),
    )(forcing, first_weight, second_weight, head_weight[None], packed)

    runoff = jnp.transpose(blocks, (1, 0, 2, 3)).reshape(step_count, tiles * band, height)
    discharge = flows[:step_count, :count].T[None]
    return (runoff, discharge)


def solution(mesh):
    placed = (
        P("tm", "tile", "grp", None),
        P(),
        P(),
        P(),
        P("grp", "tile"),
        P("tile", "grp"),
        P("tile", "grp"),
        P("tile", "grp"),
        P(("grp", "tile")),
    )
    return jax.shard_map(
        local,
        mesh=mesh,
        in_specs=placed,
        out_specs=(P("tm", "grp", "tile"), P("tile", "grp", "tm")),
        check_vma=False,
    )
```

```python
from functools import partial

import jax
import jax.numpy as jnp
from jax import lax
from jax.experimental import pallas as pl
from jax.experimental.pallas import tpu as pltpu
from jax.sharding import PartitionSpec as P

LEVELS = 8
F32 = jnp.float32
BF16 = jnp.bfloat16
VMEM_BYTES = 56 * 1024 * 1024
AHEAD = 3


def iota(shape, dim):
    return lax.broadcasted_iota(jnp.int32, shape, dim)


def as_column(row_value, count):
    spread = jnp.broadcast_to(row_value.astype(F32), (count, count))
    return jnp.sum(
        jnp.where(iota((count, count), 0) == iota((count, count), 1), spread, 0.0),
        axis=1,
        keepdims=True,
    )


def drain_kernel(codes_ref, outlets_ref, receivers_ref, inlets_ref, levels_ref, packed_ref):
    width, height = codes_ref.shape
    count = outlets_ref.shape[1]
    codes = codes_ref[...].astype(F32)
    codes = jnp.concatenate([codes, jnp.full((height - width, height), 2.0, F32)], axis=0)
    codes = codes.T.astype(jnp.int32)
    shape = (height, height)
    rows, columns = iota(shape, 0), iota(shape, 1)
    moved = columns + jnp.where(codes == 1, 1, 0) - jnp.where(codes == 3, 1, 0)
    moved = jnp.where((moved < 0) | (moved >= width), height - 1, moved)
    landing = jnp.where((rows == height - 1) | (columns >= width), columns, moved)
    reach = 1
    while reach < height:
        below = jnp.concatenate([landing[reach:], columns[:reach]], axis=0)
        landing = jnp.take_along_axis(below, landing, axis=1, mode="promise_in_bounds")
        reach *= 2
    outlet_columns = as_column(outlets_ref[...], count).astype(jnp.int32) // height
    lanes = iota((count, height), 1)
    ranked = jnp.where(
        outlet_columns >= lanes, outlet_columns * count + iota((count, height), 0), height * count
    )
    nearest = jnp.min(ranked.astype(F32), axis=0, keepdims=True).astype(jnp.int32)
    nearest = jnp.where(iota((1, height), 1) < width, nearest % count, -1)
    drained = jnp.take_along_axis(
        jnp.broadcast_to(nearest, shape), landing, axis=1, mode="promise_in_bounds"
    )
    packed_ref[:width, :] = drained.astype(F32).T[:width].astype(BF16)
    lane = iota((count, height), 1)
    table = jnp.where(lane == 0, as_column(receivers_ref[...], count), 0.0)
    inlets = jnp.maximum(as_column(inlets_ref[...], count).astype(jnp.int32), 0)
    table = jnp.where(lane == 1, (inlets // height).astype(F32), table)
    table = jnp.where(lane == 2, (inlets % height).astype(F32), table)
    table = jnp.where(lane == 3, levels_ref[0].astype(F32), table)
    packed_ref[width:, :] = table.astype(BF16)


def shifted(value):
    count = value.shape[1]
    lanes = iota(value.shape, 1)
    before = jnp.where(lanes == 0, 0.0, pltpu.roll(value, 1, 1))
    after = jnp.where(lanes == count - 1, 0.0, pltpu.roll(value, count - 1, 1))
    return before, value, after


def route_matrix(gathered_ref, width, count):
    tiles, depth, height = gathered_ref.shape
    everything = tiles * count
    table = gathered_ref[:, width:, :].reshape(everything, height).astype(F32)
    receiver = table[:, 0:1].astype(jnp.int32)
    inlet_column = table[:, 1:2].astype(jnp.int32)
    inlet_row = table[:, 2:3].astype(jnp.int32)
    sends = (receiver >= 0) & (table[:, 3:4] < LEVELS - 1.0)
    drained = gathered_ref[:, :width, :].reshape(tiles * width, height)
    picks = jnp.where(
        iota((everything, tiles * width), 1) == receiver * width + inlet_column, 1.0, 0.0
    ).astype(BF16)
    picked = jnp.dot(picks, drained, preferred_element_type=F32)
    entered = jnp.sum(
        jnp.where(iota(picked.shape, 1) == inlet_row, picked, 0.0), axis=1, keepdims=True
    ).astype(jnp.int32)
    target = jnp.where(sends & (entered >= 0), receiver * count + entered, -1)
    square = (everything, everything)
    hop = jnp.where(iota(square, 1) == target, 1.0, 0.0)
    passed = hop + jnp.where(iota(square, 0) == iota(square, 1), 1.0, 0.0)
    hops = 1
    hop = hop.astype(BF16)
    while 2 * hops < LEVELS:
        hop = jnp.dot(hop, hop, preferred_element_type=F32).astype(BF16)
        passed = passed + jnp.dot(passed.astype(BF16), hop, preferred_element_type=F32)
        hops *= 2
    return passed


def lay_out(weight_ref, out_ref, group):
    cin, cout = weight_ref.shape[2:]
    same = jnp.where(iota((cout, cout), 0) == iota((cout, cout), 1), 1.0, 0.0).astype(BF16)
    for j in range(group):
        parts = []
        for b in range(3):
            if j > 0:
                parts.append(jnp.zeros((j * cin, cout), BF16))
            parts += [weight_ref[a, b] for a in range(3)]
            if j < group - 1:
                parts.append(jnp.zeros(((group - 1 - j) * cin, cout), BF16))
        out_ref[j * cout : (j + 1) * cout, :] = lax.dot_general(
            same,
            jnp.concatenate(parts, axis=0),
            (((1,), (1,)), ((), ())),
            preferred_element_type=F32,
        ).astype(BF16)


def one_step(
    step,
    place,
    tiles,
    group1,
    group2,
    before_ref,
    forcing_ref,
    after_ref,
    w1_ref,
    w2_ref,
    head_ref,
    x_ref,
    h_ref,
):
    _, band, cin, rows = forcing_ref.shape
    channels = head_ref.shape[0]
    chunk = 256
    first = 0
    for ref in (before_ref, forcing_ref, after_ref):
        depth = ref.shape[1] * cin
        parts = shifted(ref[step].reshape(depth, rows).astype(F32))
        for b in range(3):
            x_ref[b, first : first + depth, :] = parts[b].astype(BF16)
        first += depth
    start = 0
    while start < band + 2:
        wide = min(group1, band + 2 - start)
        span = (wide + 2) * cin
        if wide == group1:
            weights = w1_ref[...]
        else:
            weights = jnp.concatenate(
                [
                    w1_ref[: wide * channels, b * (group1 + 2) * cin : b * (group1 + 2) * cin + span]
                    for b in range(3)
                ],
                axis=1,
            )
        source = jnp.concatenate(
            [x_ref[b, start * cin : start * cin + span, :] for b in range(3)], axis=0
        )
        result = jnp.maximum(jnp.dot(weights, source, preferred_element_type=F32), 0.0)
        for i in range(wide):
            piece = result[i * channels : (i + 1) * channels]
            if start + i == 0:
                piece = jnp.where(place == 0, 0.0, piece)
            if start + i == band + 1:
                piece = jnp.where(place == tiles - 1, 0.0, piece)
            parts = shifted(piece)
            at = (start + i) * channels
            for b in range(3):
                h_ref[b, at : at + channels, :] = parts[b].astype(BF16)
        start += wide
    head = jnp.concatenate([head_ref[...]] * 2, axis=1)
    span = (group2 + 2) * channels
    logits = []
    for start in range(0, band, group2):
        at = start * channels
        pieces = []
        for lane in range(0, rows, chunk):
            source = jnp.concatenate(
                [h_ref[b, at : at + span, lane : lane + chunk] for b in range(3)], axis=0
            )
            deep = jnp.maximum(jnp.dot(w2_ref[...], source, preferred_element_type=F32), 0.0)
            pieces.append(
                jnp.concatenate(
                    [
                        jnp.sum(
                            deep[i * channels : (i + 1) * channels] * head, axis=0, keepdims=True
                        )
                        for i in range(group2)
                    ],
                    axis=0,
                )
            )
        logits.append(jnp.concatenate(pieces, axis=1))
    logits = jnp.concatenate(logits, axis=0)
    soft = jnp.maximum(logits, 0.0) + jnp.log1p(jnp.exp(-jnp.abs(logits)))
    return soft.astype(BF16)


def band_sums(place, count, gathered_ref, cells_ref, s_ref):
    tiles, _, height = gathered_ref.shape
    band = s_ref.shape[0]
    steps = s_ref[...].astype(BF16)
    cells_ref[...] = gathered_ref[:, : cells_ref.shape[1], :].astype(F32)
    sums = []
    for k in range(tiles):
        left, right = [], []
        own = cells_ref[k, pl.ds(place * band, band), :].astype(jnp.int32)
        for c in range(band):
            left.append(steps[c, :, k * height : (k + 1) * height])
            right.append(
                jnp.where(iota((count, height), 0) == own[c : c + 1], 1.0, 0.0).astype(BF16)
            )
        sums.append(
            lax.dot_general(
                jnp.concatenate(left, axis=1),
                jnp.concatenate(right, axis=1),
                (((1,), (1,)), ((), ())),
                preferred_element_type=F32,
            )
        )
    return jnp.concatenate(sums, axis=1)


def main_kernel(
    count,
    group1,
    group2,
    forcing_ref,
    first_ref,
    second_ref,
    headrow_ref,
    packed_ref,
    runoff_ref,
    flow_ref,
    before_ref,
    after_ref,
    gathered_ref,
    cells_ref,
    w1_ref,
    w2_ref,
    head_ref,
    x_ref,
    h_ref,
    s_ref,
    out_ref,
    share_ref,
    landed_ref,
    halo_send,
    halo_recv,
    table_send,
    table_recv,
    runoff_send,
    runoff_recv,
    share_send,
    share_recv,
):
    place = lax.axis_index("tile")
    tiles, step_count, band, height = runoff_ref.shape
    batches = runoff_send.shape[0]
    per = step_count // batches

    def each_peer(act):
        def turn(d, carry):
            act(d, lax.rem(place + d, tiles), lax.rem(place + tiles - d, tiles))
            return carry

        lax.fori_loop(1, tiles, turn, 0)

    def remote(source, landing, send, recv, peer):
        return pltpu.make_async_remote_copy(
            src_ref=source,
            dst_ref=landing,
            send_sem=send,
            recv_sem=recv,
            device_id={"tile": peer},
            device_id_type=pl.DeviceIdType.MESH,
        )

    def halo_up(t):
        return remote(
            forcing_ref.at[t, pl.ds(band - 2, 2)],
            before_ref.at[t],
            halo_send.at[0, t],
            halo_recv.at[0, t],
            place + 1,
        )

    def halo_down(t):
        return remote(
            forcing_ref.at[t, pl.ds(0, 2)],
            after_ref.at[t],
            halo_send.at[1, t],
            halo_recv.at[1, t],
            place - 1,
        )

    def table(d, peer, slot):
        return remote(
            packed_ref, gathered_ref.at[slot], table_send.at[d], table_recv.at[d], peer
        )

    def runoff_part(g, d, peer, slot):
        return remote(
            out_ref.at[peer, pl.ds(g * per, per)],
            runoff_ref.at[slot, pl.ds(g * per, per)],
            runoff_send.at[g, d],
            runoff_recv.at[g, d],
            peer,
        )

    def share(d, peer, slot):
        return remote(
            share_ref.at[peer], landed_ref.at[slot], share_send.at[d], share_recv.at[d], peer
        )

    barrier = pltpu.get_barrier_semaphore()
    each_peer(
        lambda d, peer, source: pl.semaphore_signal(
            barrier, inc=1, device_id={"tile": peer}, device_id_type=pl.DeviceIdType.MESH
        )
    )
    pl.semaphore_wait(barrier, tiles - 1)

    def start_halos(t, carry):
        @pl.when(place < tiles - 1)
        def _():
            halo_up(t).start()

        @pl.when(place > 0)
        def _():
            halo_down(t).start()

        return carry

    lax.fori_loop(0, AHEAD, start_halos, 0)

    @pl.when(place == 0)
    def _():
        before_ref[...] = jnp.zeros_like(before_ref)

    @pl.when(place == tiles - 1)
    def _():
        after_ref[...] = jnp.zeros_like(after_ref)

    gathered_ref[place] = packed_ref[...]
    s_ref[...] = jnp.zeros_like(s_ref)
    lay_out(first_ref, w1_ref, group1)
    lay_out(second_ref, w2_ref, group2)
    channels = head_ref.shape[0]
    head_ref[...] = jnp.broadcast_to(as_column(headrow_ref[...], channels), head_ref.shape)

    def batch(g, carry):
        def turn(i, inner):
            t = g * per + i

            @pl.when(place > 0)
            def _():
                halo_up(t).wait_recv()

            @pl.when(place < tiles - 1)
            def _():
                halo_down(t).wait_recv()

            @pl.when(t + AHEAD < step_count)
            def _():
                start_halos(t + AHEAD, 0)

            rounded = one_step(
                t,
                place,
                tiles,
                group1,
                group2,
                before_ref,
                forcing_ref,
                after_ref,
                w1_ref,
                w2_ref,
                head_ref,
                x_ref,
                h_ref,
            )
            for k in range(tiles):
                out_ref[k, t] = rounded[:, k * height : (k + 1) * height]
            kept = rounded.astype(F32)
            for c in range(band):
                s_ref[c, pl.ds(t, 1), :] = kept[c : c + 1]
            return inner

        lax.fori_loop(0, per, turn, 0)
        each_peer(lambda d, peer, source: runoff_part(g, d, peer, place).start())

        @pl.when(g == batches // 2 - 1)
        def _():
            each_peer(lambda d, peer, source: table(d, peer, place).start())

        return carry

    lax.fori_loop(0, batches, batch, 0)
    runoff_ref[place] = out_ref[place]

    each_peer(lambda d, peer, source: table(d, peer, source).wait_recv())
    local_sums = band_sums(place, count, gathered_ref, cells_ref, s_ref)
    passed = route_matrix(gathered_ref, band * tiles, count)
    flows = jnp.dot(
        local_sums, passed, precision=lax.Precision.HIGHEST, preferred_element_type=F32
    )
    filler = jnp.zeros((flows.shape[0], share_ref.shape[2] - count), F32)
    for k in range(tiles):
        share_ref[k] = jnp.concatenate([flows[:, k * count : (k + 1) * count], filler], axis=1)
    each_peer(lambda d, peer, source: share(d, peer, place).start())
    landed_ref[place] = share_ref[place]
    each_peer(lambda d, peer, source: share(d, peer, source).wait_recv())
    scale = count / (band * tiles * height)
    flow_ref[...] = jnp.sum(landed_ref[...], axis=0) * scale

    def finish(g, carry):
        each_peer(lambda d, peer, source: runoff_part(g, d, peer, source).wait_recv())
        each_peer(lambda d, peer, source: runoff_part(g, d, peer, place).wait_send())
        return carry

    lax.fori_loop(0, batches, finish, 0)
    each_peer(lambda d, peer, source: share(d, peer, place).wait_send())
    each_peer(lambda d, peer, source: table(d, peer, place).wait_send())

    def end_halos(t, carry):
        @pl.when(place < tiles - 1)
        def _():
            halo_up(t).wait_send()

        @pl.when(place > 0)
        def _():
            halo_down(t).wait_send()

        return carry

    lax.fori_loop(0, step_count, end_halos, 0)


def local(
    forcing,
    first_weight,
    second_weight,
    head_weight,
    flow_codes,
    outlet_cells,
    receivers,
    inlet_cells,
    levels,
):
    tiles = lax.axis_size("tile")
    step_count, band, cin, rows = forcing.shape
    width, height = flow_codes.shape
    count = outlet_cells.shape[1]
    channels = first_weight.shape[3]
    group1, group2 = 3, min(4, band)

    packed = pl.pallas_call(
        drain_kernel,
        out_shape=jax.ShapeDtypeStruct((width + count, height), BF16),
        in_specs=[pl.BlockSpec(memory_space=pltpu.VMEM)] * 4
        + [pl.BlockSpec(memory_space=pltpu.SMEM)],
        out_specs=pl.BlockSpec(memory_space=pltpu.VMEM),
    )(flow_codes, outlet_cells, receivers, inlet_cells, levels)
    padded_steps = -(-step_count // 16) * 16
    batches = step_count // 3 if step_count % 3 == 0 else step_count
    dma = pltpu.SemaphoreType.DMA
    vmem = pl.BlockSpec(memory_space=pltpu.VMEM)
    blocks, flows = pl.pallas_call(
        partial(main_kernel, count, group1, group2),
        in_specs=[vmem] * 5,
        out_shape=(
            jax.ShapeDtypeStruct((tiles, step_count, band, height), BF16),
            jax.ShapeDtypeStruct((padded_steps, 128), F32),
        ),
        out_specs=(vmem, vmem),
        scratch_shapes=[
            pltpu.VMEM((step_count, 2, cin, rows), BF16),
            pltpu.VMEM((step_count, 2, cin, rows), BF16),
            pltpu.VMEM((tiles, width + count, height), BF16),
            pltpu.VMEM((tiles, width, height), F32),
            pltpu.VMEM((group1 * channels, 3 * (group1 + 2) * cin), BF16),
            pltpu.VMEM((group2 * channels, 3 * (group2 + 2) * channels), BF16),
            pltpu.VMEM((channels, 128), F32),
            pltpu.VMEM((3, (band + 4) * cin, rows), BF16),
            pltpu.VMEM((3, (band + 2) * channels, rows), BF16),
            pltpu.VMEM((band, padded_steps, rows), F32),
            pltpu.VMEM((tiles, step_count, band, height), BF16),
            pltpu.VMEM((tiles, padded_steps, 128), F32),
            pltpu.VMEM((tiles, padded_steps, 128), F32),
            dma((2, step_count)),
            dma((2, step_count)),
            dma((tiles,)),
            dma((tiles,)),
            dma((batches, tiles)),
            dma((batches, tiles)),
            dma((tiles,)),
            dma((tiles,)),
        ],
        compiler_params=pltpu.CompilerParams(
            collective_id=0, has_side_effects=True, vmem_limit_bytes=VMEM_BYTES
        ),
    )(forcing, first_weight, second_weight, head_weight[None], packed)

    runoff = jnp.transpose(blocks, (1, 0, 2, 3)).reshape(step_count, tiles * band, height)
    discharge = flows[:step_count, :count].T[None]
    return (runoff, discharge)


def solution(mesh):
    placed = (
        P("tm", "tile", "grp", None),
        P(),
        P(),
        P(),
        P("grp", "tile"),
        P("tile", "grp"),
        P("tile", "grp"),
        P("tile", "grp"),
        P(("grp", "tile")),
    )
    return jax.shard_map(
        local,
        mesh=mesh,
        in_specs=placed,
        out_specs=(P("tm", "grp", "tile"), P("tile", "grp", "tm")),
        check_vma=False,
    )
```
